32 devices in a mesh: layer: 4 (over z), row: 2 (over x), col: 4 (over y, core).
Axes of the slice: x: 2, y: 2, z: 4, core: 2. Of those that a mesh axis runs over, the one named last changes fastest.
Arguments:
- density: float32 [1024, 1024], P(('row', 'col'), 'layer'), as said below
- pattern: int32 [8, 8], replicated, may hold values from 0 to 1, as said below
Outputs:
- purified: float32 [1024, 1024], P(('row', 'col'), 'layer')
The draws below stay inside these ranges and needn't reach their ends.
Inputs may be any that keep to these rules, and one draw needn't show every extreme that they name: pattern is symmetric, its diagonal is all ones. density is symmetric.
All inputs are finite; a program needn't handle non-finite values.
Results may differ from the reference program's by a relative error of at most 0.00013.
Values sent between devices are 32-bit elements; how exact they have to be, the bound alone decides.
A program may use at most 64 MiB of HBM per device.

```python
import jax
import jax.numpy as jnp
from jax import lax

TILE = 128
TILES = 8
ORDER = 1024


def draw_density(key, part):
    first = jax.random.fold_in(key, 11)
    second = jax.random.fold_in(key, 12)
    noise = jax.random.normal(first, (ORDER, ORDER), jnp.float32)
    spread = 0.3 / jnp.sqrt(ORDER / 2.0)
    symmetric = (noise + noise.T) * (spread / jnp.sqrt(2.0))
    diagonal = jax.random.uniform(second, (ORDER,), jnp.float32, 0.2, 0.8)
    return symmetric + jnp.diag(diagonal)


def draw_pattern(key, part):
    scores = jax.random.randint(jax.random.fold_in(key, 21), (TILES, TILES), 0, 100)
    index = jnp.arange(TILES, dtype=jnp.int32)
    first = index[:, None]
    second = index[None, :]
    bound = 15 + 70 * (first + second) // (2 * (TILES - 1))
    upper = (scores < bound).astype(jnp.int32)
    both = jnp.where(first <= second, upper, upper.T)
    both = jnp.where(first == second, 1, both)
    corner = (first == 0) & (second == TILES - 1) | (first == TILES - 1) & (second == 0)
    return jnp.where(corner, 0, both).astype(jnp.int32)


def setup_inputs(seed: int = 0) -> dict:
    splits = jax.random.split(jax.random.key(seed), 3)
    density = draw_density(jax.random.fold_in(splits[2], 71), 0)
    pattern = draw_pattern(jax.random.fold_in(splits[2], 71), 0)
    return dict(density=density, pattern=pattern)


def reference(density, pattern):
    keep = pattern.astype(density.dtype)
    mask = jnp.repeat(jnp.repeat(keep, TILE, axis=0), TILE, axis=1)
    masked = density * mask
    square = jnp.dot(masked, masked, precision=lax.Precision.HIGHEST, preferred_element_type=jnp.float32)
    cube = jnp.dot(square, masked, precision=lax.Precision.HIGHEST, preferred_element_type=jnp.float32)
    return 3.0 * square - 2.0 * cube
```

```python
import functools
import itertools

import jax
import jax.numpy as jnp
from jax import lax
from jax.experimental import pallas as pl
from jax.experimental.pallas import tpu as pltpu
from jax.sharding import PartitionSpec as P

TILE = 128
PAIR = 2


def split(value):
    high = value.astype(jnp.bfloat16)
    return high, (value - high.astype(jnp.float32)).astype(jnp.bfloat16)


def times(left, right):
    dot = functools.partial(jnp.dot, preferred_element_type=jnp.float32)
    return dot(left[0], right[0]) + (dot(left[0], right[1]) + dot(left[1], right[0]))


def kernel(
    layers, rows, cols, density_ref, pattern_ref, out_ref,
    panel, square, slabs, slab_sem, slab_send, panel_sem, panel_send,
):
    layer, row, col = (lax.axis_index(name) for name in ("layer", "row", "col"))
    height, width = density_ref.shape
    me = row * cols + col
    half = lax.rem(col, PAIR)
    mate_col = col + 1 - 2 * half
    mate = row * cols + mate_col
    groups = cols // PAIR
    offsets = sorted(itertools.product(range(rows), range(groups)), key=lambda at: -sum(map(bool, at)))
    offsets.remove((0, 0))

    def peer(dr, dc):
        return lax.rem(row + dr + rows, rows), lax.rem(col + PAIR * dc + cols, cols)

    barrier = pltpu.get_barrier_semaphore()

    def greet(**device):
        pl.semaphore_signal(barrier, inc=1, device_id=device, device_id_type=pl.DeviceIdType.MESH)

    greet(col=mate_col)
    for dr, dc in offsets:
        r, c = peer(dr, dc)
        greet(row=r, col=c)
    for step in range(1, layers):
        greet(layer=lax.rem(layer + step, layers))

    def block(buffer, index):
        return buffer.at[pl.ds(pl.multiple_of(index * height, height), height), :]

    own = block(panel, me)
    for i in range(height // TILE):
        for j in range(width // TILE):
            keep = pattern_ref[me * (height // TILE) + i, layer * (width // TILE) + j].astype(jnp.float32)
            part = (slice(i * TILE, (i + 1) * TILE), slice(j * TILE, (j + 1) * TILE))
            own[part] = density_ref[part] * keep

    pl.semaphore_wait(barrier, layers + len(offsets))

    def copy(source, target, send, recv, **device):
        return pltpu.make_async_remote_copy(
            src_ref=source, dst_ref=target, send_sem=send, recv_sem=recv,
            device_id=device, device_id_type=pl.DeviceIdType.MESH,
        )

    started = []

    def start(*args, **device):
        one = copy(*args, **device)
        one.start()
        started.append(one)

    def send_slabs():
        for step in range(1, layers):
            to = lax.rem(layer + step, layers)
            start(own, slabs.at[layer], slab_send.at[step - 1], slab_sem.at[layer], layer=to)

    def send_block(phase, buffer):
        mine = block(buffer, me)
        for k, (dr, dc) in enumerate(offsets):
            r, c = peer(dr, dc)
            start(mine, mine, panel_send.at[phase, k], panel_sem.at[phase, me], row=r, col=c)
        start(mine, mine, panel_send.at[phase, len(offsets)], panel_sem.at[phase, me], col=mate_col)

    def arrive(phase, buffer, index):
        there = block(buffer, index)
        copy(there, there, panel_send.at[phase, 0], panel_sem.at[phase, index], col=mate_col).wait_recv()

    def share(phase, buffer):
        for k, (dr, dc) in enumerate(reversed(offsets)):
            r, c = peer(-dr, -dc)
            source = r * cols + c
            arrive(phase, buffer, source)
            there = block(buffer, source)
            start(
                there, there, panel_send.at[phase, len(offsets) + 1 + k], panel_sem.at[phase, source],
                col=mate_col,
            )

    def collect(phase, buffer):
        arrive(phase, buffer, mate)
        for dr, dc in reversed(offsets):
            r, c = peer(-dr, -dc)
            arrive(phase, buffer, r * cols + c + 1 - 2 * half)

    def slab_of(buffer, index):
        return buffer[pl.ds(pl.multiple_of(index * width, width), width), :]

    send_block(0, panel)
    send_slabs()
    share(0, panel)
    slabs[layer] = own[...]
    collect(0, panel)
    total = times(split(own[...]), split(slab_of(panel, layer)))
    for step in range(1, layers):
        source = lax.rem(layer + layers - step, layers)
        here = slabs.at[source]
        copy(here, here, slab_send.at[0], slab_sem.at[source], layer=source).wait_recv()
        total += times(split(here[...]), split(slab_of(panel, source)))
    block(square, me)[...] = total
    send_block(1, square)
    share(1, square)
    collect(1, square)
    cube = times(split(slabs[0]), split(square[:width, :]))
    for index in range(1, layers):
        cube += times(split(slabs[index]), split(square[index * width : (index + 1) * width, :]))
    out_ref[...] = 3.0 * total - 2.0 * cube
    for one in started:
        one.wait_send()


def solution(mesh):
    layers, rows, cols = (mesh.shape[name] for name in ("layer", "row", "col"))

    def on_device(density, pattern):
        height, width = density.shape
        blocks = rows * cols
        sends = 2 * (blocks // PAIR)
        return pl.pallas_call(
            functools.partial(kernel, layers, rows, cols),
            out_shape=jax.ShapeDtypeStruct((height, width), jnp.float32),
            in_specs=[
                pl.BlockSpec(memory_space=pltpu.VMEM),
                pl.BlockSpec(memory_space=pltpu.SMEM),
            ],
            out_specs=pl.BlockSpec(memory_space=pltpu.VMEM),
            scratch_shapes=[
                pltpu.VMEM((blocks * height, width), jnp.float32),
                pltpu.VMEM((blocks * height, width), jnp.float32),
                pltpu.VMEM((layers, height, width), jnp.float32),
                pltpu.SemaphoreType.DMA((layers,)),
                pltpu.SemaphoreType.DMA((layers,)),
                pltpu.SemaphoreType.DMA((2, blocks)),
                pltpu.SemaphoreType.DMA((2, sends)),
            ],
            compiler_params=pltpu.CompilerParams(
                collective_id=0, has_side_effects=True, vmem_limit_bytes=40 * 2**20
            ),
        )(density, pattern)

    return jax.shard_map(
        on_device,
        mesh=mesh,
        in_specs=(P(("row", "col"), "layer"), P()),
        out_specs=P(("row", "col"), "layer"),
        check_vma=False,
    )
```

```python
import functools
import itertools

import jax
import jax.numpy as jnp
from jax import lax
from jax.experimental import pallas as pl
from jax.experimental.pallas import tpu as pltpu
from jax.sharding import PartitionSpec as P

TILE = 128
CHUNKS = 1
REACH = 2
PAIR = 2


def split(value):
    high = value.astype(jnp.bfloat16)
    return high, (value - high.astype(jnp.float32)).astype(jnp.bfloat16)


def times(left, right):
    dot = functools.partial(jnp.dot, preferred_element_type=jnp.float32)
    return dot(left[0], right[0]) + (dot(left[0], right[1]) + dot(left[1], right[0]))


def kernel(
    layers, rows, cols, density_hbm, pattern_hbm, out_ref,
    density_ref, pattern_ref, panel, square, slabs,
    local_sem, slab_sem, slab_send, relay_send, panel_sem, panel_send,
):
    layer, row, col = (lax.axis_index(name) for name in ("layer", "row", "col"))
    height, width = density_ref.shape
    rise = height // CHUNKS
    me = row * cols + col
    half = lax.rem(col, PAIR)
    mate_col = col + 1 - 2 * half
    mate = row * cols + mate_col
    groups = cols // PAIR
    offsets = sorted(itertools.product(range(rows), range(groups)), key=lambda at: -sum(map(bool, at)))
    offsets.remove((0, 0))

    def peer(dr, dc):
        return lax.rem(row + dr + rows, rows), lax.rem(col + PAIR * dc + cols, cols)

    load = pltpu.make_async_copy(density_hbm, density_ref, local_sem.at[0])
    load.start()
    load_pattern = pltpu.make_async_copy(pattern_hbm, pattern_ref, local_sem.at[1])
    load_pattern.start()

    barrier = pltpu.get_barrier_semaphore()

    def greet(**device):
        pl.semaphore_signal(barrier, inc=1, device_id=device, device_id_type=pl.DeviceIdType.MESH)

    def inside(at):
        return (at >= 0) & (at < layers)

    reach = [sign * far for far in range(min(REACH, layers - 1), 0, -1) for sign in (1, -1)]
    known = jnp.int32(1 + len(offsets))
    greet(col=mate_col)
    for away in reach:
        pl.when(inside(layer + away))(functools.partial(greet, layer=layer + away))
        known += inside(layer + away).astype(jnp.int32)
    for dr, dc in offsets:
        r, c = peer(dr, dc)
        greet(row=r, col=c)

    def block(buffer, index):
        return buffer.at[pl.ds(pl.multiple_of(index * height, height), height), :]

    def piece(buffer, index, chunk):
        return buffer.at[pl.ds(pl.multiple_of(index * height + chunk * rise, rise), rise), :]

    own = block(panel, me)
    load_pattern.wait()
    load.wait()
    for i in range(height // TILE):
        for j in range(width // TILE):
            keep = pattern_ref[me * (height // TILE) + i, layer * (width // TILE) + j].astype(jnp.float32)
            part = (slice(i * TILE, (i + 1) * TILE), slice(j * TILE, (j + 1) * TILE))
            own[part] = density_ref[part] * keep

    pl.semaphore_wait(barrier, known)

    def copy(source, target, send, recv, **device):
        return pltpu.make_async_remote_copy(
            src_ref=source, dst_ref=target, send_sem=send, recv_sem=recv,
            device_id=device, device_id_type=pl.DeviceIdType.MESH,
        )

    started = []

    def start(when, *args, **device):
        one = copy(*args, **device)
        if when is None:
            one.start()
        else:
            pl.when(when)(one.start)
        started.append((when, one))

    def chunk_of(chunk):
        return pl.ds(chunk * rise, rise)

    def send_slab(chunk):
        for n, away in enumerate(reach):
            start(
                inside(layer + away),
                piece(panel, me, chunk), slabs.at[layer, chunk_of(chunk)],
                slab_send.at[chunk, n], slab_sem.at[chunk, layer], layer=layer + away,
            )

    def slab_arrives(chunk, source):
        there = slabs.at[source, chunk_of(chunk)]
        copy(there, there, slab_send.at[0, 0], slab_sem.at[chunk, source], layer=layer).wait_recv()

    relays = [(sign, hops) for hops in range(1, (layers - 2) // REACH + 1) for sign in (1, -1)]

    def relay_slab(chunk):
        for n, (sign, hops) in enumerate(relays):
            source = layer - sign * hops * REACH
            mine = inside(source) & inside(layer + sign)
            pl.when(mine)(functools.partial(slab_arrives, chunk, source))
            for far in range(REACH, 0, -1):
                there = slabs.at[source, chunk_of(chunk)]
                start(
                    inside(source) & inside(layer + sign * far),
                    there, there, relay_send.at[chunk, n, far - 1], slab_sem.at[chunk, source],
                    layer=layer + sign * far,
                )

    def relayed(source):
        below = (source < layer) & (layer + 1 < layers)
        above = (source > layer) & (layer > 0)
        return (lax.rem(lax.abs(source - layer), REACH) == 0) & (below | above)

    def send_piece(phase, mine):
        for k, (dr, dc) in enumerate(offsets):
            r, c = peer(dr, dc)
            start(None, mine, mine, panel_send.at[phase, k], panel_sem.at[phase, me], row=r, col=c)
        start(None, mine, mine, panel_send.at[phase, len(offsets)], panel_sem.at[phase, me], col=mate_col)

    def arrive(phase, there, index):
        copy(there, there, panel_send.at[phase, 0], panel_sem.at[phase, index], col=mate_col).wait_recv()

    def share(phase, at):
        for k, (dr, dc) in enumerate(reversed(offsets)):
            r, c = peer(-dr, -dc)
            source = r * cols + c
            there = at(source)
            arrive(phase, there, source)
            start(
                None, there, there, panel_send.at[phase, len(offsets) + 1 + k],
                panel_sem.at[phase, source], col=mate_col,
            )

    def collect(phase, at):
        arrive(phase, at(mate), mate)
        for dr, dc in reversed(offsets):
            r, c = peer(-dr, -dc)
            source = r * cols + c + 1 - 2 * half
            arrive(phase, at(source), source)

    def slab_of(buffer, index):
        return buffer[pl.ds(pl.multiple_of(index * width, width), width), :]

    whole = functools.partial(block, panel)
    parts = [functools.partial(piece, square, chunk=chunk) for chunk in range(CHUNKS)]

    send_slab(0)
    send_piece(0, own)
    for chunk in range(1, CHUNKS):
        send_slab(chunk)
    slabs[layer] = own[...]
    relay_slab(0)
    share(0, whole)
    for chunk in range(1, CHUNKS - 1):
        relay_slab(chunk)
    collect(0, whole)
    for chunk in range(CHUNKS):
        if 0 < chunk == CHUNKS - 1:
            relay_slab(chunk)
        total = times(split(slabs[layer, chunk_of(chunk)]), split(slab_of(panel, layer)))
        for step in range(1, layers):
            source = lax.rem(layer + layers - step, layers)
            pl.when(jnp.logical_not(relayed(source)))(functools.partial(slab_arrives, chunk, source))
            total += times(split(slabs[source, chunk_of(chunk)]), split(slab_of(panel, source)))
        piece(square, me, chunk)[...] = total
        send_piece(1 + chunk, piece(square, me, chunk))
        if chunk:
            share(chunk, parts[chunk - 1])
    share(CHUNKS, parts[-1])
    for chunk in range(CHUNKS):
        collect(1 + chunk, parts[chunk])
    cube = times(split(slabs[0]), split(square[:width, :]))
    for index in range(1, layers):
        cube += times(split(slabs[index]), split(square[index * width : (index + 1) * width, :]))
    out_ref[...] = 3.0 * block(square, me)[...] - 2.0 * cube
    for when, one in started:
        if when is None:
            one.wait_send()
        else:
            pl.when(when)(one.wait_send)


def solution(mesh):
    layers, rows, cols = (mesh.shape[name] for name in ("layer", "row", "col"))

    def on_device(density, pattern):
        height, width = density.shape
        blocks = rows * cols
        sends = 2 * (blocks // PAIR)
        return pl.pallas_call(
            functools.partial(kernel, layers, rows, cols),
            out_shape=jax.ShapeDtypeStruct((height, width), jnp.float32),
            in_specs=[
                pl.BlockSpec(memory_space=pltpu.HBM),
                pl.BlockSpec(memory_space=pltpu.HBM),
            ],
            out_specs=pl.BlockSpec(memory_space=pltpu.VMEM),
            scratch_shapes=[
                pltpu.VMEM((height, width), jnp.float32),
                pltpu.SMEM(pattern.shape, jnp.int32),
                pltpu.VMEM((blocks * height, width), jnp.float32),
                pltpu.VMEM((blocks * height, width), jnp.float32),
                pltpu.VMEM((layers, height, width), jnp.float32),
                pltpu.SemaphoreType.DMA((2,)),
                pltpu.SemaphoreType.DMA((CHUNKS, layers)),
                pltpu.SemaphoreType.DMA((CHUNKS, 2 * REACH)),
                pltpu.SemaphoreType.DMA((CHUNKS, layers, REACH)),
                pltpu.SemaphoreType.DMA((1 + CHUNKS, blocks)),
                pltpu.SemaphoreType.DMA((1 + CHUNKS, sends)),
            ],
            compiler_params=pltpu.CompilerParams(
                collective_id=0, has_side_effects=True, vmem_limit_bytes=40 * 2**20
            ),
        )(density, pattern)

    return jax.shard_map(
        on_device,
        mesh=mesh,
        in_specs=(P(("row", "col"), "layer"), P()),
        out_specs=P(("row", "col"), "layer"),
        check_vma=False,
    )
```

```python
import functools
import itertools

import jax
import jax.numpy as jnp
from jax import lax
from jax.experimental import pallas as pl
from jax.experimental.pallas import tpu as pltpu
from jax.sharding import PartitionSpec as P

TILE = 128
CHUNKS = 1
REACH = 2
PAIR = 2


def split(value):
    high = value.astype(jnp.bfloat16)
    return high, (value - high.astype(jnp.float32)).astype(jnp.bfloat16)


def times(left, right):
    dot = functools.partial(jnp.dot, preferred_element_type=jnp.float32)
    return dot(left[0], right[0]) + (dot(left[0], right[1]) + dot(left[1], right[0]))


def kernel(
    layers, rows, cols, density_hbm, pattern_hbm, out_ref,
    density_ref, pattern_ref, panel, square, slabs,
    local_sem, slab_sem, slab_send, relay_send, panel_sem, panel_send,
):
    layer, row, col = (lax.axis_index(name) for name in ("layer", "row", "col"))
    height, width = density_ref.shape
    rise = height // CHUNKS
    me = row * cols + col
    half = lax.rem(col, PAIR)
    mate_col = col + 1 - 2 * half
    mate = row * cols + mate_col
    groups = cols // PAIR
    offsets = sorted(itertools.product(range(rows), range(groups)), key=lambda at: -sum(map(bool, at)))
    offsets.remove((0, 0))

    def peer(dr, dc):
        return lax.rem(row + dr + rows, rows), lax.rem(col + PAIR * dc + cols, cols)

    load = pltpu.make_async_copy(density_hbm, density_ref, local_sem.at[0])
    load.start()
    load_pattern = pltpu.make_async_copy(pattern_hbm, pattern_ref, local_sem.at[1])
    load_pattern.start()

    barrier = pltpu.get_barrier_semaphore()

    def greet(**device):
        pl.semaphore_signal(barrier, inc=1, device_id=device, device_id_type=pl.DeviceIdType.MESH)

    def inside(at):
        return (at >= 0) & (at < layers)

    reach = [sign * far for far in range(min(REACH, layers - 1), 0, -1) for sign in (1, -1)]
    known = jnp.int32(1 + len(offsets))
    greet(col=mate_col)
    for away in reach:
        pl.when(inside(layer + away))(functools.partial(greet, layer=layer + away))
        known += inside(layer + away).astype(jnp.int32)
    for dr, dc in offsets:
        r, c = peer(dr, dc)
        greet(row=r, col=c)

    def block(buffer, index):
        return buffer.at[pl.ds(pl.multiple_of(index * height, height), height), :]

    def piece(buffer, index, chunk):
        return buffer.at[pl.ds(pl.multiple_of(index * height + chunk * rise, rise), rise), :]

    own = block(panel, me)
    load_pattern.wait()
    load.wait()
    for i in range(height // TILE):
        for j in range(width // TILE):
            keep = pattern_ref[me * (height // TILE) + i, layer * (width // TILE) + j].astype(jnp.float32)
            part = (slice(i * TILE, (i + 1) * TILE), slice(j * TILE, (j + 1) * TILE))
            own[part] = density_ref[part] * keep

    pl.semaphore_wait(barrier, known)

    def copy(source, target, send, recv, **device):
        return pltpu.make_async_remote_copy(
            src_ref=source, dst_ref=target, send_sem=send, recv_sem=recv,
            device_id=device, device_id_type=pl.DeviceIdType.MESH,
        )

    started = []

    def start(when, *args, **device):
        one = copy(*args, **device)
        if when is None:
            one.start()
        else:
            pl.when(when)(one.start)
        started.append((when, one))

    def chunk_of(chunk):
        return pl.ds(chunk * rise, rise)

    def send_slab(chunk):
        for n, away in enumerate(reach):
            start(
                inside(layer + away),
                piece(panel, me, chunk), slabs.at[layer, chunk_of(chunk)],
                slab_send.at[chunk, n], slab_sem.at[chunk, layer], layer=layer + away,
            )

    def slab_arrives(chunk, source):
        there = slabs.at[source, chunk_of(chunk)]
        copy(there, there, slab_send.at[0, 0], slab_sem.at[chunk, source], layer=layer).wait_recv()

    relays = [(sign, hops) for hops in range(1, (layers - 2) // REACH + 1) for sign in (1, -1)]

    def relay_slab(chunk):
        for n, (sign, hops) in enumerate(relays):
            source = layer - sign * hops * REACH
            mine = inside(source) & inside(layer + sign)
            pl.when(mine)(functools.partial(slab_arrives, chunk, source))
            for far in range(REACH, 0, -1):
                there = slabs.at[source, chunk_of(chunk)]
                start(
                    inside(source) & inside(layer + sign * far),
                    there, there, relay_send.at[chunk, n, far - 1], slab_sem.at[chunk, source],
                    layer=layer + sign * far,
                )

    def relayed(source):
        below = (source < layer) & (layer + 1 < layers)
        above = (source > layer) & (layer > 0)
        return (lax.rem(lax.abs(source - layer), REACH) == 0) & (below | above)

    def send_piece(phase, mine):
        for k, (dr, dc) in enumerate(offsets):
            r, c = peer(dr, dc)
            start(None, mine, mine, panel_send.at[phase, k], panel_sem.at[phase, me], row=r, col=c)
        start(None, mine, mine, panel_send.at[phase, len(offsets)], panel_sem.at[phase, me], col=mate_col)

    def arrive(phase, there, index):
        copy(there, there, panel_send.at[phase, 0], panel_sem.at[phase, index], col=mate_col).wait_recv()

    def share(phase, at):
        for k, (dr, dc) in enumerate(reversed(offsets)):
            r, c = peer(-dr, -dc)
            source = r * cols + c
            there = at(source)
            arrive(phase, there, source)
            start(
                None, there, there, panel_send.at[phase, len(offsets) + 1 + k],
                panel_sem.at[phase, source], col=mate_col,
            )

    def collect(phase, at):
        arrive(phase, at(mate), mate)
        for dr, dc in reversed(offsets):
            r, c = peer(-dr, -dc)
            source = r * cols + c + 1 - 2 * half
            arrive(phase, at(source), source)

    def slab_of(buffer, index):
        return buffer[pl.ds(pl.multiple_of(index * width, width), width), :]

    whole = functools.partial(block, panel)
    parts = [functools.partial(piece, square, chunk=chunk) for chunk in range(CHUNKS)]

    send_slab(0)
    send_piece(0, own)
    for chunk in range(1, CHUNKS):
        send_slab(chunk)
    slabs[layer] = own[...]
    relay_slab(0)
    share(0, whole)
    for chunk in range(1, CHUNKS - 1):
        relay_slab(chunk)
    collect(0, whole)
    for chunk in range(CHUNKS):
        if 0 < chunk == CHUNKS - 1:
            relay_slab(chunk)
        total = times(split(slabs[layer, chunk_of(chunk)]), split(slab_of(panel, layer)))
        for step in range(1, layers):
            source = lax.rem(layer + layers - step, layers)
            pl.when(jnp.logical_not(relayed(source)))(functools.partial(slab_arrives, chunk, source))
            total += times(split(slabs[source, chunk_of(chunk)]), split(slab_of(panel, source)))
        piece(square, me, chunk)[...] = total
        send_piece(1 + chunk, piece(square, me, chunk))
        if chunk:
            share(chunk, parts[chunk - 1])
    def term(first):
        left = jnp.concatenate(
            [
                slabs[lax.div(first + n, width // height), :, pl.ds(pl.multiple_of(lax.rem(first + n, width // height) * height, TILE), height)]
                for n in range(PAIR)
            ],
            axis=1,
        )
        return times(split(left), split(square[pl.ds(pl.multiple_of(first * height, height), PAIR * height), :]))

    for chunk in range(CHUNKS):
        arrive(1 + chunk, parts[chunk](mate), mate)
    cube = term(me - half)
    share(CHUNKS, parts[-1])
    for dr, dc in reversed(offsets):
        r, c = peer(-dr, -dc)
        source = r * cols + c + 1 - 2 * half
        for chunk in range(CHUNKS):
            arrive(1 + chunk, parts[chunk](source), source)
        cube += term(r * cols + c - half)
    out_ref[...] = 3.0 * block(square, me)[...] - 2.0 * cube
    for when, one in started:
        if when is None:
            one.wait_send()
        else:
            pl.when(when)(one.wait_send)


def solution(mesh):
    layers, rows, cols = (mesh.shape[name] for name in ("layer", "row", "col"))

    def on_device(density, pattern):
        height, width = density.shape
        blocks = rows * cols
        sends = 2 * (blocks // PAIR)
        return pl.pallas_call(
            functools.partial(kernel, layers, rows, cols),
            out_shape=jax.ShapeDtypeStruct((height, width), jnp.float32),
            in_specs=[
                pl.BlockSpec(memory_space=pltpu.HBM),
                pl.BlockSpec(memory_space=pltpu.HBM),
            ],
            out_specs=pl.BlockSpec(memory_space=pltpu.VMEM),
            scratch_shapes=[
                pltpu.VMEM((height, width), jnp.float32),
                pltpu.SMEM(pattern.shape, jnp.int32),
                pltpu.VMEM((blocks * height, width), jnp.float32),
                pltpu.VMEM((blocks * height, width), jnp.float32),
                pltpu.VMEM((layers, height, width), jnp.float32),
                pltpu.SemaphoreType.DMA((2,)),
                pltpu.SemaphoreType.DMA((CHUNKS, layers)),
                pltpu.SemaphoreType.DMA((CHUNKS, 2 * REACH)),
                pltpu.SemaphoreType.DMA((CHUNKS, layers, REACH)),
                pltpu.SemaphoreType.DMA((1 + CHUNKS, blocks)),
                pltpu.SemaphoreType.DMA((1 + CHUNKS, sends)),
            ],
            compiler_params=pltpu.CompilerParams(
                collective_id=0, has_side_effects=True, vmem_limit_bytes=40 * 2**20
            ),
        )(density, pattern)

    return jax.shard_map(
        on_device,
        mesh=mesh,
        in_specs=(P(("row", "col"), "layer"), P()),
        out_specs=P(("row", "col"), "layer"),
        check_vma=False,
    )
```
